256 devices in a mesh: dp: 64 (over z_lo, y, x, core), tensor: 4 (over z_hi).
Axes of the slice: x: 4, y: 4, z: 8 (z_hi: 4, z_lo: 2; z = z_hi * 2 + z_lo), core: 2. Of those that a mesh axis runs over, the one named last changes fastest.
Arguments:
- acts: bfloat16 [8192, 8192], P('dp', 'tensor'), may hold values from -6 to 6
- gate_pre: bfloat16 [8192, 28672], P('dp', 'tensor'), may hold values from -8 to 8
- up_pre: bfloat16 [8192, 28672], P('dp', 'tensor'), may hold values from -6 to 6
- hidden_cot: bfloat16 [8192, 28672], P('dp', 'tensor'), may hold values from -6 to 6
- out_cot: bfloat16 [8192, 8192], P('dp', 'tensor'), may hold values from -6 to 6
- proj_model: bfloat16 [64, 8192], P(None, 'tensor'), may hold values from -0.0625 to 0.0625
- proj_hidden: bfloat16 [64, 28672], P(None, 'tensor'), may hold values from -0.03125 to 0.03125
- stored: bfloat16 [65024, 12288], P('dp', 'tensor'), may hold values from -6 to 6
- queries: bfloat16 [1024, 12288], P('dp', 'tensor'), may hold values from -0.0546875 to 0.0546875
- slots: int32 [512], P('dp'), may hold values from 0 to 511, as said below
Outputs:
- new_index: bfloat16 [512, 12288], P('dp', 'tensor')
- scores: float32 [65536, 1024], P(('dp', 'tensor'))
The draws below stay inside these ranges and needn't reach their ends.
Inputs may be any that keep to these rules, and one draw needn't show every extreme that they name: slots is a permutation; entry e equals 8 times its owner block plus e % 8, and the 8 sequences of one dp index have different owner blocks.
All inputs are finite; a program needn't handle non-finite values.
Results may differ from the reference program's by a relative error of at most 0.014.
Values may be sent and summed in bfloat16 or wider, within the bound.
A program may use at most 128 MiB of HBM per device.

```python
import jax
import jax.numpy as jnp
from jax import lax

D = 8192
FF = 28672
RANK = 64
SEQ_DEV = 8
TOK_DEV = 128
WIN = 16
FEAT = 12288
STORE_DEV = 1016
TOKENS = 8192
NEW = 512
NQ = 1024
STORE = 65024
ALL = 65536
N_DP = 64


def draw_slots(key, part):
    key = jax.random.fold_in(key, 7)
    blocks = NEW // SEQ_DEV
    first_key, second_key = jax.random.split(key)
    mapping = jax.random.permutation(first_key, blocks)
    shifts = jax.random.permutation(second_key, blocks)[:SEQ_DEV]
    owners = (mapping[:, None] + shifts[None, :]) % blocks
    result = owners * SEQ_DEV + jnp.arange(SEQ_DEV, dtype=jnp.int32)[None, :]
    return result.reshape(-1).astype(jnp.int32)


def levels(own_key, shape, cuts, low, high):
    gain = 1.0
    for position, parts in cuts:
        heights = jax.random.uniform(jax.random.fold_in(jax.random.fold_in(own_key, 6), position), (parts,), jnp.float32, low / len(cuts), high / len(cuts))
        gain = gain * jnp.repeat(jnp.exp(heights), shape[position] // parts).reshape((-1,) + (1,) * (len(shape) - 1 - position))
    return gain


def gaussian(key, dims, spread, reach, cuts=(), held_as=jnp.bfloat16):
    array = spread * jax.random.normal(key, dims, jnp.float32)
    if cuts:
        array = array * levels(key, dims, cuts, -0.22, 0.18)
    return jnp.clip(array, -reach, reach).astype(held_as)


def setup_inputs(seed: int = 0) -> dict:
    keys = jax.random.split(jax.random.key(seed), 11)
    acts = gaussian(keys[0], (TOKENS, D), 1.0, 6.0, ((0, 64), (1, 4)))
    gate_pre = gaussian(keys[1], (TOKENS, FF), 1.5, 8.0, ((0, 64), (1, 4)))
    up_pre = gaussian(keys[2], (TOKENS, FF), 1.0, 6.0, ((0, 64), (1, 4)))
    hidden_cot = gaussian(keys[3], (TOKENS, FF), 1.0, 6.0, ((0, 64), (1, 4)))
    out_cot = gaussian(keys[4], (TOKENS, D), 1.0, 6.0, ((0, 64), (1, 4)))
    proj_model = gaussian(keys[5], (RANK, D), D ** -0.5, 0.0625, ((1, 4),))
    proj_hidden = gaussian(keys[6], (RANK, FF), FF ** -0.5, 0.03125, ((1, 4),))
    stored = gaussian(keys[7], (STORE, FEAT), 1.0, 6.0, ((0, 64), (1, 4)))
    queries = gaussian(keys[8], (NQ, FEAT), FEAT ** -0.5, 0.0546875, ((0, 64), (1, 4)))
    slots = draw_slots(jax.random.fold_in(keys[10], 71), 0)
    return dict(acts=acts, gate_pre=gate_pre, up_pre=up_pre, hidden_cot=hidden_cot, out_cot=out_cot, proj_model=proj_model, proj_hidden=proj_hidden, stored=stored, queries=queries, slots=slots)


def token_factors(operands, proj_model, proj_hidden):
    acts, gate_pre, up_pre, hidden_cot, out_cot = operands
    gate_float = gate_pre.astype(jnp.float32)
    up_float = up_pre.astype(jnp.float32)
    cot_float = hidden_cot.astype(jnp.float32)
    sigma = jax.nn.sigmoid(gate_float)
    silu_gate = gate_float * sigma
    hidden = (silu_gate * up_float).astype(jnp.bfloat16)
    up_cot = (cot_float * silu_gate).astype(jnp.bfloat16)
    gate_cot = (cot_float * up_float * sigma * (1.0 + gate_float * (1.0 - sigma))).astype(jnp.bfloat16)
    in_model = jnp.dot(acts, proj_model.T, preferred_element_type=jnp.float32)
    gate_side = jnp.dot(gate_cot, proj_hidden.T, preferred_element_type=jnp.float32)
    up_side = jnp.dot(up_cot, proj_hidden.T, preferred_element_type=jnp.float32)
    in_hidden = jnp.dot(hidden, proj_hidden.T, preferred_element_type=jnp.float32)
    down_side = jnp.dot(out_cot, proj_model.T, preferred_element_type=jnp.float32)
    return jnp.stack([in_model, gate_side, up_side, in_hidden, down_side], axis=1)


def reference(acts, gate_pre, up_pre, hidden_cot, out_cot, proj_model, proj_hidden, stored, queries, slots):
    blocks = N_DP

    def one_block(operands):
        return token_factors(operands, proj_model, proj_hidden)

    operands = (acts.reshape(blocks, TOK_DEV, D), gate_pre.reshape(blocks, TOK_DEV, FF),
                up_pre.reshape(blocks, TOK_DEV, FF), hidden_cot.reshape(blocks, TOK_DEV, FF),
                out_cot.reshape(blocks, TOK_DEV, D))
    factors = lax.map(one_block, operands)
    factors = factors.reshape(NEW, WIN, 5, RANK)
    gate_grad = jnp.einsum("ewi,ewj->eij", factors[:, :, 0], factors[:, :, 1])
    up_grad = jnp.einsum("ewi,ewj->eij", factors[:, :, 0], factors[:, :, 2])
    down_grad = jnp.einsum("ewi,ewj->eij", factors[:, :, 3], factors[:, :, 4])
    gradients = jnp.concatenate([gate_grad.reshape(NEW, RANK * RANK), up_grad.reshape(NEW, RANK * RANK),
                                 down_grad.reshape(NEW, RANK * RANK)], axis=1).astype(jnp.bfloat16)
    new_index = jnp.zeros((NEW, FEAT), jnp.bfloat16).at[slots.astype(jnp.int32)].set(gradients)
    index = jnp.concatenate([stored.reshape(blocks, STORE_DEV, FEAT),
                             new_index.reshape(blocks, SEQ_DEV, FEAT)], axis=1).reshape(ALL, FEAT)
    scores = jnp.dot(index, queries.T, preferred_element_type=jnp.float32)
    return new_index, scores
```

```python
import jax
import jax.numpy as jnp
from jax import lax
from jax.experimental import pallas as pl
from jax.experimental.pallas import tpu as pltpu
from jax.sharding import PartitionSpec as P

MESH = pl.DeviceIdType.MESH
BF16, F32 = jnp.bfloat16, jnp.float32
RANK = 64
SHARD = 16
ROWS = 256
NQ = 1024
FEAT = 3072
HALF = FEAT // 2
PIECE = HALF + 128
TILE = 512
FLANES = 384


def product(left, right):
    return lax.dot_general(left, right, (((1,), (1,)), ((), ())), preferred_element_type=F32)


def iota(shape, dim):
    return lax.broadcasted_iota(jnp.int32, shape, dim)


class Place:
    def __init__(self):
        dp = lax.axis_index("dp")
        self.dp, self.t = dp, lax.axis_index("tensor")
        self.core = dp % 2
        self.x, self.y, self.zl = (dp // 2) % 4, (dp // 8) % 4, dp // 32
        self.a = self.x + self.core * (self.y - self.x)
        self.b = self.y + self.core * (self.x - self.y)

    def at(self, a, b, zl):
        x = a + self.core * (b - a)
        y = b + self.core * (a - b)
        return (((zl * 4 + y) * 4 + x) * 2 + self.core, self.t)

    def sibling(self):
        return (self.dp + 1 - 2 * self.core, self.t)

    def z_partner(self):
        return self.at(self.a, self.b, 1 - self.zl)

    def a_peer(self, k):
        return self.at((self.a + k) % 4, self.b, self.zl)

    def b_peer(self, k):
        return self.at(self.a, (self.b + k) % 4, self.zl)

    def tensor(self, k):
        return (self.dp, (self.t + k) % 4)


def slot(core, zl, b, a):
    return ((core * 2 + zl) * 4 + b) * 4 + a


class Gather:
    def __init__(self, me, panel, send, recv):
        self.me, self.panel, self.send, self.recv = me, panel, send, recv
        self.count = 0
        self.copies = []

    def copy(self, start, size, device):
        i = self.count
        self.count += 1
        part = self.panel.at[pl.ds(start, size)]
        made = pltpu.make_async_remote_copy(
            src_ref=part, dst_ref=part, send_sem=self.send.at[i], recv_sem=self.recv.at[i],
            device_id=device, device_id_type=MESH)
        made.start()
        self.copies.append(made)
        return made

    def own(self):
        me = self.me
        mine = slot(me.core, me.zl, me.b, me.a)
        self.sib0 = self.copy(mine, 1, me.sibling())
        self.a0 = [self.copy(mine, 1, me.a_peer(k)) for k in (1, 3, 2)]
        self.z = self.copy(mine, 1, me.z_partner())

    def after_z(self):
        me = self.me
        self.z.wait_recv()
        mine = slot(me.core, 1 - me.zl, me.b, me.a)
        self.a1 = [self.copy(mine, 1, me.a_peer(k)) for k in (1, 3, 2)]

    def after_a0(self):
        me = self.me
        self.sib_a0 = []
        for made, k in zip(self.a0, (1, 3, 2)):
            made.wait_recv()
            self.sib_a0.append(self.copy(slot(me.core, me.zl, me.b, (me.a + 4 - k) % 4), 1, me.sibling()))
        row = slot(me.core, me.zl, me.b, 0)
        self.b0 = [self.copy(row, 4, me.b_peer(k)) for k in (1, 3, 2)]

    def after_a1(self):
        me = self.me
        for made in self.a1:
            made.wait_recv()
        row = slot(me.core, 1 - me.zl, me.b, 0)
        self.sib_a1 = self.copy(row, 4, me.sibling())
        self.b1 = [self.copy(row, 4, me.b_peer(k)) for k in (1, 3, 2)]
        self.sib_b = {}

    def after_b(self, far, i):
        me = self.me
        k = (1, 3, 2)[i]
        (self.b1 if far else self.b0)[i].wait_recv()
        zl = 1 - me.zl if far else me.zl
        self.sib_b[far, i] = self.copy(slot(me.core, zl, (me.b + 4 - k) % 4, 0), 4, me.sibling())

    def finish(self):
        for made in self.copies:
            made.wait_send()


GATHER_COPIES = 1 + 3 + 1 + 3 + 3 + 3 + 1 + 3 + 6


def chunks(me):
    c, z, a, b = me.core, me.zl, me.a, me.b
    far = 1 - z
    result = [[(c, z, b, a, 1), (1 - c, z, a, b, 1)]]
    back = [3, 1, 2]
    result.append([(c, z, b, (a + k) % 4, 1) for k in back] + [(1 - c, z, a, (b + k) % 4, 1) for k in back])
    result.append([(c, far, b, 0, 4), (1 - c, far, a, 0, 4)])
    for zl in (z, far):
        for k in back:
            result.append([(c, zl, (b + k) % 4, 0, 4), (1 - c, zl, (a + k) % 4, 0, 4)])
    return result


CHUNK_ROWS = [32, 96] + [128] * 7
CHUNK_AT = [sum(CHUNK_ROWS[:i]) for i in range(len(CHUNK_ROWS))]
N_CHUNKS = len(CHUNK_ROWS)


def kernel(acts_hbm, gate_hbm, up_hbm, cot_hbm, outc_hbm, pm_hbm, ph_hbm, stored_hbm, queries_hbm, slots_ref,
           new_ref, out_ref,
           acts, gate, up, cot, outc, pm, ph, stored, panel, gpanel,
           acc, fac, fac_in, hsend, hrecv, g32,
           s1p, s1m, r1p, r1m, s2p, s2m, r2p, r2m, pp, pm_part, po, nsend, nrecv,
           local_sem, q_send, q_recv, g_send, g_recv, rs_send, rs_recv, f_send, f_recv, h_send, h_recv, n_send, n_recv):
    me = Place()
    t = me.t

    mine = slot(me.core, me.zl, me.b, me.a)
    own_q = pltpu.make_async_copy(queries_hbm, panel.at[mine], local_sem.at[0])
    own_q.start()
    stored_in = [
        pltpu.make_async_copy(stored_hbm.at[pl.ds(256 * i, 256 if i < 3 else 248)],
                              stored.at[pl.ds(256 * i, 256 if i < 3 else 248)], local_sem.at[1 + i])
        for i in range(4)
    ]
    stored[1008:, :] = jnp.zeros((16, FEAT), BF16)
    for made in stored_in:
        made.start()
    hidden_in = [pltpu.make_async_copy(src, dst, local_sem.at[5 + i]) for i, (src, dst) in enumerate(
        [(gate_hbm, gate), (up_hbm, up), (cot_hbm, cot), (ph_hbm, ph), (acts_hbm, acts), (outc_hbm, outc), (pm_hbm, pm)])]
    for made in hidden_in:
        made.start()

    barrier = pltpu.get_barrier_semaphore()
    partners = [me.sibling(), me.z_partner()]
    for k in (1, 2, 3):
        partners += [me.a_peer(k), me.b_peer(k), me.tensor(k)]
    for device in partners:
        pl.semaphore_signal(barrier, inc=1, device_id=device, device_id_type=MESH)
    pl.semaphore_wait(barrier, len(partners))

    gather = Gather(me, panel, q_send, q_recv)
    own_q.wait()
    gather.own()
    for made in stored_in:
        made.wait()

    parts = chunks(me)
    blocks = [(t + k) % 4 for k in range(4)]
    rs_copies = []

    def rs_copy(src, dst, rows, index, k):
        made = pltpu.make_async_remote_copy(
            src_ref=src.at[rows], dst_ref=dst.at[rows], send_sem=rs_send.at[index], recv_sem=rs_recv.at[index],
            device_id=me.tensor(k), device_id_type=MESH)
        made.start()
        rs_copies.append(made)
        return made

    def score(i, block):
        total = None
        for column in range(0, FEAT, TILE):
            left = jnp.concatenate(
                [panel[pl.ds(slot(c, zl, b, a), n), :, column:column + TILE].reshape(n * SHARD, TILE)
                 for c, zl, b, a, n in parts[i]], axis=0)
            right = stored[pl.ds(pl.multiple_of(block * ROWS, ROWS), ROWS), column:column + TILE]
            term = product(left, right)
            total = term if total is None else total + term
        return total

    first, second = {}, {}

    def stage1(i):
        rows = pl.ds(CHUNK_AT[i], CHUNK_ROWS[i])
        part = score(i, blocks[2]).astype(BF16)
        s1p[rows, :] = part[:, :128]
        s1m[rows, :] = part[:, 128:]
        first[i] = (rs_copy(s1p, r1p, rows, 4 * i, 1), rs_copy(s1m, r1m, rows, 4 * i + 1, 3))
        pp[rows, :] = score(i, blocks[1])
        pm_part[rows, :] = score(i, blocks[3])
        po[rows, :] = score(i, blocks[0])

    def stage2(i):
        rows = pl.ds(CHUNK_AT[i], CHUNK_ROWS[i])
        s2p[rows, 128:] = pp[rows, 128:].astype(BF16)
        s2m[rows, :128] = pm_part[rows, :128].astype(BF16)
        first[i][0].wait_recv()
        s2p[rows, :128] = (pp[rows, :128] + r1p[rows, :].astype(F32)).astype(BF16)
        plus = rs_copy(s2p, r2p, rows, 4 * i + 2, 1)
        first[i][1].wait_recv()
        s2m[rows, 128:] = (pm_part[rows, 128:] + r1m[rows, :].astype(F32)).astype(BF16)
        minus = rs_copy(s2m, r2m, rows, 4 * i + 3, 3)
        second[i] = (plus, minus)

    def stage3(i):
        for made in second[i]:
            made.wait_recv()
        at = CHUNK_AT[i]
        for c, zl, b, a, n in parts[i]:
            for j in range(n):
                rows = pl.ds(at, SHARD)
                value = po[rows, :] + r2p[rows, :].astype(F32) + r2m[rows, :].astype(F32)
                x = (a + j) + c * (b - (a + j))
                y = b + c * ((a + j) - b)
                place = ((zl * 4 + y) * 4 + x) * 2 + c
                out_ref[pl.ds(pl.multiple_of(place * SHARD, SHARD), SHARD), :] = value
                at += SHARD

    def factors_part(begin, end):
        def step(i, total):
            columns = pl.ds(pl.multiple_of(i * TILE, TILE), TILE)
            g = gate[:, columns].astype(F32)
            u = up[:, columns].astype(F32)
            c = cot[:, columns].astype(F32)
            s = jax.nn.sigmoid(g)
            silu = g * s
            hidden = (silu * u).astype(BF16)
            up_cot = (c * silu).astype(BF16)
            gate_cot = (c * u * s * (1.0 + g * (1.0 - s))).astype(BF16)
            return total + product(jnp.concatenate([gate_cot, up_cot, hidden], axis=0), ph[:, columns])

        acc[...] += lax.fori_loop(begin, end, step, jnp.zeros((384, RANK), F32))

    fac_copies, h_copies = [], []

    def factors_send():
        model = product(jnp.concatenate([acts[...], outc[...]], axis=0), pm[...]).astype(BF16)
        hidden = acc[...].astype(BF16)
        row, lane = iota((RANK, FLANES), 0), iota((RANK, FLANES), 1)
        split = (row % 2) * 32 + row // 2

        def spread(value, target):
            return jnp.dot(value, (lane == target).astype(F32).astype(BF16), preferred_element_type=F32)

        fac[...] = (spread(model[:128], split) + spread(hidden[256:], split + 64) + spread(hidden[:128], row + 128)
                    + spread(hidden[128:256], row + 192) + spread(model[128:], row + 256)).astype(BF16)
        for k in (1, 2, 3):
            made = pltpu.make_async_remote_copy(
                src_ref=fac.at[pl.ds(pl.multiple_of(32 * blocks[k], 32), 32)], dst_ref=fac_in.at[k - 1],
                send_sem=f_send.at[k - 1], recv_sem=f_recv.at[k - 1],
                device_id=me.tensor(k), device_id_type=MESH)
            made.start()
            fac_copies.append(made)

    def gradients():
        total = fac[pl.ds(pl.multiple_of(32 * t, 32), 32), :].astype(F32)
        for k in (1, 2, 3):
            fac_copies[k - 1].wait_recv()
            total += fac_in[k - 1].astype(F32)
        low = iota((32, 128), 1) < RANK
        both = []
        for s in range(2):
            one = total[16 * s:16 * s + 16]
            outer = lax.dot_general(one[:, :128], one[:, 128:], (((0,), (0,)), ((), ())),
                                    precision=lax.Precision.HIGHEST, preferred_element_type=F32)
            m_even, m_odd = outer[:32, :128], outer[32:64, :128]
            h_even, h_odd = outer[64:96, 128:], outer[96:, 128:]
            both.append(jnp.concatenate([
                jnp.where(low, m_even, pltpu.roll(m_odd, 64, 1)),
                jnp.where(low, pltpu.roll(m_even, 64, 1), m_odd),
                jnp.where(low, h_even, pltpu.roll(h_odd, 64, 1))], axis=0))
        for k in range(4):
            hsend[k] = jnp.concatenate([both[0][24 * k:24 * k + 24], both[1][24 * k:24 * k + 24]], axis=0).astype(BF16)
        for k in (1, 2, 3):
            made = pltpu.make_async_remote_copy(
                src_ref=hsend.at[blocks[k]], dst_ref=hrecv.at[k - 1], send_sem=h_send.at[k - 1],
                recv_sem=h_recv.at[k - 1], device_id=me.tensor(k), device_id_type=MESH)
            made.start()
            h_copies.append(made)

    def shard():
        g32[pl.ds(pl.multiple_of(48 * t, 48), 48), :] = hsend[t].astype(F32)
        for k in (1, 2, 3):
            h_copies[k - 1].wait_recv()
            g32[pl.ds(pl.multiple_of(48 * ((t + 4 - k) % 4), 48), 48), :] = hrecv[k - 1].astype(F32)
        for k in range(12):
            gpanel[mine, :, 128 * k:128 * k + 128] = jnp.concatenate(
                [g32[pl.ds(k, 8, stride=24), :], g32[pl.ds(k + 12, 8, stride=24), :]], axis=0).astype(BF16)
        sequence = iota((SHARD, 128), 0) % 8
        owner = jnp.zeros((SHARD, 128), F32)
        for j in range(8):
            owner = jnp.where(sequence == j, (slots_ref[j] // 8).astype(F32), owner)
        gpanel[mine, :, HALF:] = owner.astype(BF16)

    n_copies = []

    def new_rows():
        total = jnp.zeros((128, HALF), F32)
        shape = (256, 128)
        right_row = (iota(shape, 0) % SHARD) == iota(shape, 1)
        number = me.dp.astype(F32)
        for i in range(4):
            part = gpanel[pl.ds(16 * i, 16)].reshape(256, PIECE)
            owner = part[:, HALF:].astype(F32)
            pick = jnp.where(jnp.logical_and(right_row, owner == number), 1.0, 0.0).astype(BF16)
            total += lax.dot_general(pick, part[:, :HALF], (((0,), (0,)), ((), ())), preferred_element_type=F32)
        rows = jnp.concatenate([total[:8], total[8:16]], axis=1)
        new_ref[...] = rows.astype(BF16)
        left = jnp.concatenate([rows, rows], axis=0).astype(BF16)
        halves = []
        for c in range(2):
            halves.append(jnp.concatenate(
                [product(left, panel[pl.ds(32 * c + 8 * i, 8)].reshape(128, FEAT))[:8] for i in range(4)], axis=1))
        nsend[...] = jnp.concatenate(halves, axis=0).astype(BF16)
        for k in (1, 2, 3):
            n_copies.append(pltpu.make_async_remote_copy(
                src_ref=nsend, dst_ref=nrecv.at[k - 1], send_sem=n_send.at[k - 1],
                recv_sem=n_recv.at[k - 1], device_id=me.tensor(k), device_id_type=MESH))
        for k in (1, 2, 3):
            @pl.when((t + k) % 4 == 3)
            def _():
                n_copies[k - 1].start()

    def new_scores():
        @pl.when(t == 3)
        def _():
            for made in n_copies:
                made.wait_recv()
            total = nsend[...].astype(F32)
            for k in range(3):
                total += nrecv[k].astype(F32)
            for c in range(2):
                turned = jnp.transpose(jnp.concatenate(
                    [jnp.zeros((120, 512), F32), total[8 * c:8 * c + 8]], axis=0))
                for zl in range(2):
                    for b in range(4):
                        for a in range(4):
                            x, y = (a, b) if c == 0 else (b, a)
                            place = ((zl * 4 + y) * 4 + x) * 2 + c
                            at = ((zl * 4 + b) * 4 + a) * SHARD
                            out_ref[place * SHARD:(place + 1) * SHARD, 128:] += turned[at:at + SHARD]
        for k in (1, 2, 3):
            @pl.when((t + k) % 4 == 3)
            def _():
                n_copies[k - 1].wait_send()

    acc[...] = jnp.zeros_like(acc)
    grads = Gather(me, gpanel, g_send, g_recv)

    gather.sib0.wait_recv()
    stage1(0)
    gather.after_a0()
    gather.after_z()
    for made in gather.sib_a0:
        made.wait_recv()
    stage1(1)
    stage2(0)
    for made in hidden_in:
        made.wait()
    factors_part(0, 7)
    gather.after_a1()
    stage2(1)
    gather.sib_a1.wait_recv()
    stage1(2)
    factors_part(7, 14)
    factors_send()
    stage2(2)
    gather.after_b(False, 0)
    gather.after_b(False, 1)
    gather.sib_b[False, 0].wait_recv()
    stage1(3)
    gradients()
    gather.sib_b[False, 1].wait_recv()
    stage1(4)
    stage2(3)
    shard()
    grads.own()
    gather.after_b(False, 2)
    gather.sib_b[False, 2].wait_recv()
    stage1(5)
    stage2(4)
    grads.after_a0()
    grads.after_z()
    gather.after_b(True, 0)
    gather.sib_b[True, 0].wait_recv()
    stage1(6)
    stage2(5)
    gather.after_b(True, 1)
    gather.sib_b[True, 1].wait_recv()
    stage1(7)
    grads.after_a1()
    stage2(6)
    gather.after_b(True, 2)
    gather.sib_b[True, 2].wait_recv()
    stage1(8)
    stage2(7)
    stage3(0)
    stage3(1)
    for far in (False, True):
        for i in range(3):
            grads.after_b(far, i)
    stage3(2)
    stage2(8)
    grads.sib0.wait_recv()
    for made in grads.sib_a0:
        made.wait_recv()
    grads.sib_a1.wait_recv()
    for far in (False, True):
        for i in range(3):
            grads.sib_b[far, i].wait_recv()
    new_rows()
    for i in range(3, N_CHUNKS):
        stage3(i)
    new_scores()

    gather.finish()
    grads.finish()
    for made in rs_copies + fac_copies + h_copies:
        made.wait_send()


def body(acts, gate_pre, up_pre, hidden_cot, out_cot, proj_model, proj_hidden, stored, queries, slots):
    tokens, model = acts.shape
    hidden = gate_pre.shape[1]
    vmem = pltpu.VMEM
    dma = pltpu.SemaphoreType.DMA
    new_block, turned = pl.pallas_call(
        kernel,
        out_shape=(jax.ShapeDtypeStruct((8, FEAT), BF16), jax.ShapeDtypeStruct((NQ, ROWS), F32)),
        in_specs=[pl.BlockSpec(memory_space=pl.ANY)] * 9 + [pl.BlockSpec(memory_space=pltpu.SMEM)],
        out_specs=(pl.BlockSpec(memory_space=pltpu.VMEM), pl.BlockSpec(memory_space=pltpu.VMEM)),
        scratch_shapes=[
            vmem((tokens, model), BF16), vmem((tokens, hidden), BF16), vmem((tokens, hidden), BF16),
            vmem((tokens, hidden), BF16), vmem((tokens, model), BF16), vmem((RANK, model), BF16),
            vmem((RANK, hidden), BF16), vmem((4 * ROWS, FEAT), BF16), vmem((64, SHARD, FEAT), BF16),
            vmem((64, SHARD, PIECE), BF16),
            vmem((384, RANK), F32), vmem((128, FLANES), BF16), vmem((3, 32, FLANES), BF16),
            vmem((4, 48, 128), BF16), vmem((3, 48, 128), BF16), vmem((192, 128), F32),
            vmem((NQ, 128), BF16), vmem((NQ, 128), BF16), vmem((NQ, 128), BF16), vmem((NQ, 128), BF16),
            vmem((NQ, ROWS), BF16), vmem((NQ, ROWS), BF16), vmem((NQ, ROWS), BF16), vmem((NQ, ROWS), BF16),
            vmem((NQ, ROWS), F32), vmem((NQ, ROWS), F32), vmem((NQ, ROWS), F32),
            vmem((SHARD, 512), BF16), vmem((3, SHARD, 512), BF16),
            dma((12,)), dma((GATHER_COPIES,)), dma((GATHER_COPIES,)), dma((GATHER_COPIES,)), dma((GATHER_COPIES,)),
            dma((4 * N_CHUNKS,)), dma((4 * N_CHUNKS,)), dma((3,)), dma((3,)), dma((3,)), dma((3,)), dma((3,)), dma((3,)),
        ],
        compiler_params=pltpu.CompilerParams(
            collective_id=0, has_side_effects=True, vmem_limit_bytes=56 * 2**20),
    )(acts, gate_pre, up_pre, hidden_cot, out_cot, proj_model, proj_hidden, stored, queries, slots)
    return new_block, turned.T


def solution(mesh):
    return jax.shard_map(
        body,
        mesh=mesh,
        in_specs=(
            P("dp", "tensor"), P("dp", "tensor"), P("dp", "tensor"), P("dp", "tensor"), P("dp", "tensor"),
            P(None, "tensor"), P(None, "tensor"), P("dp", "tensor"), P("dp", "tensor"), P("dp"),
        ),
        out_specs=(P("dp", "tensor"), P(("dp", "tensor"), None)),
        check_vma=False,
    )
```

```python
import jax
import jax.numpy as jnp
from jax import lax
from jax.experimental import pallas as pl
from jax.experimental.pallas import tpu as pltpu
from jax.sharding import PartitionSpec as P

MESH = pl.DeviceIdType.MESH
BF16, F32 = jnp.bfloat16, jnp.float32
RANK = 64
SHARD = 16
ROWS = 256
NQ = 1024
FEAT = 3072
HALF = FEAT // 2
PIECE = HALF + 128
TILE = 512
FLANES = 384


def product(left, right):
    return lax.dot_general(left, right, (((1,), (1,)), ((), ())), preferred_element_type=F32)


def iota(shape, dim):
    return lax.broadcasted_iota(jnp.int32, shape, dim)


class Place:
    def __init__(self):
        dp = lax.axis_index("dp")
        self.dp, self.t = dp, lax.axis_index("tensor")
        self.core = dp % 2
        self.x, self.y, self.zl = (dp // 2) % 4, (dp // 8) % 4, dp // 32
        self.a = self.x + self.core * (self.y - self.x)
        self.b = self.y + self.core * (self.x - self.y)

    def at(self, a, b, zl):
        x = a + self.core * (b - a)
        y = b + self.core * (a - b)
        return (((zl * 4 + y) * 4 + x) * 2 + self.core, self.t)

    def sibling(self):
        return (self.dp + 1 - 2 * self.core, self.t)

    def z_partner(self):
        return self.at(self.a, self.b, 1 - self.zl)

    def a_peer(self, k):
        return self.at((self.a + k) % 4, self.b, self.zl)

    def b_peer(self, k):
        return self.at(self.a, (self.b + k) % 4, self.zl)

    def tensor(self, k):
        return (self.dp, (self.t + k) % 4)

    def queries_of(self, p, z, b, a):
        core = self.core + p * (1 - 2 * self.core)
        first, second = (self.a, self.b) if p == 0 else (self.b, self.a)
        a_at, b_at, z_at = (first + a) % 4, (second + b) % 4, (self.zl + z) % 2
        x = a_at + core * (b_at - a_at)
        y = b_at + core * (a_at - b_at)
        return ((z_at * 4 + y) * 4 + x) * 2 + core


def slot(p, z, b, a):
    return ((p * 2 + z) * 4 + b) * 4 + a


class Gather:
    def __init__(self, me, panel, send, recv):
        self.me, self.panel, self.send, self.recv = me, panel, send, recv
        self.count = 0
        self.copies, self.landing, self.landed = [], {}, set()

    def copy(self, source, target, device, size=1):
        i = self.count
        self.count += 1
        made = pltpu.make_async_remote_copy(
            src_ref=self.panel.at[pl.ds(slot(*source), size)], dst_ref=self.panel.at[pl.ds(slot(*target), size)],
            send_sem=self.send.at[i], recv_sem=self.recv.at[i], device_id=device, device_id_type=MESH)
        made.start()
        self.copies.append(made)
        for j in range(size):
            self.landing[slot(*target) + j] = i

    def wait(self, *places):
        for place in places:
            i = self.landing[slot(*place)]
            if i not in self.landed:
                self.landed.add(i)
                self.copies[i].wait_recv()

    def to_sibling(self, z, b, a, size=1):
        self.copy((0, z, b, a), (1, z, b, a), self.me.sibling(), size)

    def along_a(self, z, k):
        self.copy((0, z, 0, 0), (0, z, 0, 4 - k), self.me.a_peer(k))

    def along_b(self, z, a):
        for k in (1, 3):
            self.copy((0, z, 0, a), (0, z, 4 - k, a), self.me.b_peer(k))

    def start(self):
        self.to_sibling(0, 0, 0)
        self.along_a(0, 1)
        self.along_a(0, 3)
        self.along_b(0, 0)
        self.copy((0, 0, 0, 0), (0, 1, 0, 0), self.me.z_partner())
        self.along_a(0, 2)

    def on_z(self):
        self.wait((0, 1, 0, 0))
        self.along_a(1, 1)
        self.along_a(1, 3)
        self.along_b(1, 0)
        self.along_a(1, 2)
        self.to_sibling(1, 0, 0)

    def on_a(self, z, a):
        self.wait((0, z, 0, a))
        self.along_b(z, a)
        self.to_sibling(z, 0, a)

    def on_b(self, z, a):
        for b in (1, 3):
            self.wait((0, z, b, a))
            self.to_sibling(z, b, a)

    def pass_on(self, z, low):
        if low:
            self.copy((0, z, 3, 0), (0, z, 2, 0), self.me.b_peer(1), 2)
        else:
            self.copy((0, z, 1, 2), (0, z, 2, 2), self.me.b_peer(3), 2)

    def on_opposite(self, z):
        self.wait((0, z, 2, 0), (0, z, 2, 2))
        self.to_sibling(z, 2, 0, 4)

    def finish(self):
        for made in self.copies:
            made.wait_send()


GATHER_COPIES = 7 + 9 + 6 + 9 + 16 + 4 + 2

CHUNKS = [
    [(0, 0, 0, 0), (1, 0, 0, 0), (0, 0, 0, 1), (0, 0, 0, 3), (1, 0, 0, 1), (1, 0, 0, 3), (0, 0, 1, 0), (0, 0, 3, 0)],
    [(0, 0, 0, 2), (1, 0, 0, 2), (0, 0, 1, 1), (0, 0, 3, 1), (0, 0, 1, 3), (0, 0, 3, 3), (1, 0, 1, 0), (1, 0, 3, 0)],
    [(0, 1, 0, 0), (1, 1, 0, 0), (0, 1, 0, 1), (0, 1, 0, 3), (1, 1, 0, 1), (1, 1, 0, 3), (0, 0, 1, 2), (0, 0, 3, 2)],
    [(1, 0, b, a) for b in (1, 3) for a in (1, 2, 3)] + [(0, 1, 0, 2), (1, 1, 0, 2), (0, 1, 1, 0), (0, 1, 3, 0)],
    [(p, 0, 2, a) for p in (0, 1) for a in range(4)] + [(0, 1, b, a) for b in (1, 3) for a in (1, 2, 3)],
    [(1, 1, b, a) for b in (1, 3) for a in range(4)] + [(p, 1, 2, a) for p in (0, 1) for a in range(4)],
]
CHUNK_ROWS = [SHARD * len(parts) for parts in CHUNKS]
CHUNK_AT = [sum(CHUNK_ROWS[:i]) for i in range(len(CHUNK_ROWS))]
N_CHUNKS = len(CHUNK_ROWS)


def kernel(acts_hbm, gate_hbm, up_hbm, cot_hbm, outc_hbm, pm_hbm, ph_hbm, stored_hbm, queries_hbm, slots_ref,
           new_ref, out_ref,
           acts, gate, up, cot, outc, pm, ph, stored, panel, gpanel,
           acc, fac, fac_in, hsend, hrecv, g32,
           send, recv, pp, pm_part, po, nsend, nrecv,
           local_sem, q_send, q_recv, g_send, g_recv, rs_send, rs_recv, f_send, f_recv, h_send, h_recv, n_send, n_recv):
    me = Place()
    t = me.t

    mine = 0
    own_q = pltpu.make_async_copy(queries_hbm, panel.at[mine], local_sem.at[0])
    own_q.start()
    stored_in = [
        pltpu.make_async_copy(stored_hbm.at[pl.ds(256 * i, 256 if i < 3 else 248)],
                              stored.at[pl.ds(256 * i, 256 if i < 3 else 248)], local_sem.at[1 + i])
        for i in range(4)
    ]
    stored[1008:, :] = jnp.zeros((16, FEAT), BF16)
    hidden_in = [pltpu.make_async_copy(src, dst, local_sem.at[5 + i]) for i, (src, dst) in enumerate(
        [(gate_hbm, gate), (up_hbm, up), (cot_hbm, cot), (ph_hbm, ph), (acts_hbm, acts), (outc_hbm, outc), (pm_hbm, pm)])]

    for made in hidden_in:
        made.start()

    barrier = pltpu.get_barrier_semaphore()
    partners = [me.sibling(), me.z_partner()]
    for k in (1, 2, 3):
        partners += [me.a_peer(k), me.b_peer(k), me.tensor(k)]
    for device in partners:
        pl.semaphore_signal(barrier, inc=1, device_id=device, device_id_type=MESH)
    pl.semaphore_wait(barrier, len(partners))

    gather = Gather(me, panel, q_send, q_recv)
    own_q.wait()
    gather.start()

    blocks = [(t + k) % 4 for k in range(4)]
    rs_copies = []

    def rs_copy(i, kind, k):
        rows = pl.ds(CHUNK_AT[i], CHUNK_ROWS[i])
        made = pltpu.make_async_remote_copy(
            src_ref=send.at[kind, rows], dst_ref=recv.at[kind, rows], send_sem=rs_send.at[6 * i + kind],
            recv_sem=rs_recv.at[6 * i + kind], device_id=me.tensor(k), device_id_type=MESH)
        made.start()
        rs_copies.append(made)
        reduce[i, kind] = made

    def score(i, block):
        total = None
        for column in range(0, FEAT, TILE):
            left = jnp.concatenate(
                [panel[slot(*place), :, column:column + TILE] for place in CHUNKS[i]], axis=0)
            right = stored[pl.ds(pl.multiple_of(block * ROWS, ROWS), ROWS), column:column + TILE]
            term = product(left, right)
            total = term if total is None else total + term
        return total

    reduce = {}

    def stage1(i):
        rows = pl.ds(CHUNK_AT[i], CHUNK_ROWS[i])
        part = score(i, blocks[2])
        send[0, rows, :] = part[:, :128].astype(BF16)
        rs_copy(i, 0, 1)
        send[1, rows, :] = part[:, 128:].astype(BF16)
        rs_copy(i, 1, 3)
        part = score(i, blocks[1])
        send[2, rows, :] = part[:, 128:].astype(BF16)
        rs_copy(i, 2, 1)
        pp[rows, :] = part[:, :128]
        part = score(i, blocks[3])
        send[3, rows, :] = part[:, :128].astype(BF16)
        rs_copy(i, 3, 3)
        pm_part[rows, :] = part[:, 128:]
        po[rows, :] = score(i, blocks[0])

    def stage2(i):
        rows = pl.ds(CHUNK_AT[i], CHUNK_ROWS[i])
        reduce[i, 0].wait_recv()
        send[4, rows, :] = (pp[rows, :] + recv[0, rows, :].astype(F32)).astype(BF16)
        rs_copy(i, 4, 1)
        reduce[i, 1].wait_recv()
        send[5, rows, :] = (pm_part[rows, :] + recv[1, rows, :].astype(F32)).astype(BF16)
        rs_copy(i, 5, 3)

    def stage3(i):
        for kind in (2, 3, 4, 5):
            reduce[i, kind].wait_recv()
        for j, place in enumerate(CHUNKS[i]):
            rows = pl.ds(CHUNK_AT[i] + SHARD * j, SHARD)
            target = pl.ds(pl.multiple_of(me.queries_of(*place) * SHARD, SHARD), SHARD)
            out_ref[target, :128] = po[rows, :128] + recv[3, rows, :].astype(F32) + recv[4, rows, :].astype(F32)
            out_ref[target, 128:] = po[rows, 128:] + recv[2, rows, :].astype(F32) + recv[5, rows, :].astype(F32)

    def factors_part(begin, end):
        def step(i, total):
            columns = pl.ds(pl.multiple_of(i * TILE, TILE), TILE)
            g = gate[:, columns].astype(F32)
            u = up[:, columns].astype(F32)
            c = cot[:, columns].astype(F32)
            s = jax.nn.sigmoid(g)
            silu = g * s
            hidden = (silu * u).astype(BF16)
            up_cot = (c * silu).astype(BF16)
            gate_cot = (c * u * s * (1.0 + g * (1.0 - s))).astype(BF16)
            return total + product(jnp.concatenate([gate_cot, up_cot, hidden], axis=0), ph[:, columns])

        acc[...] += lax.fori_loop(begin, end, step, jnp.zeros((384, RANK), F32))

    fac_copies, h_copies = [], []

    def factors_send():
        model = product(jnp.concatenate([acts[...], outc[...]], axis=0), pm[...]).astype(BF16)
        hidden = acc[...].astype(BF16)
        row, lane = iota((RANK, FLANES), 0), iota((RANK, FLANES), 1)
        split = (row % 2) * 32 + row // 2

        def spread(value, target):
            return jnp.dot(value, (lane == target).astype(F32).astype(BF16), preferred_element_type=F32)

        fac[...] = (spread(model[:128], split) + spread(hidden[256:], split + 64) + spread(hidden[:128], row + 128)
                    + spread(hidden[128:256], row + 192) + spread(model[128:], row + 256)).astype(BF16)
        for k in (1, 2, 3):
            made = pltpu.make_async_remote_copy(
                src_ref=fac.at[pl.ds(pl.multiple_of(32 * blocks[k], 32), 32)], dst_ref=fac_in.at[k - 1],
                send_sem=f_send.at[k - 1], recv_sem=f_recv.at[k - 1],
                device_id=me.tensor(k), device_id_type=MESH)
            made.start()
            fac_copies.append(made)

    def gradients():
        total = fac[pl.ds(pl.multiple_of(32 * t, 32), 32), :].astype(F32)
        for k in (1, 2, 3):
            fac_copies[k - 1].wait_recv()
            total += fac_in[k - 1].astype(F32)
        low = iota((32, 128), 1) < RANK
        both = []
        for s in range(2):
            one = total[16 * s:16 * s + 16]
            outer = lax.dot_general(one[:, :128], one[:, 128:], (((0,), (0,)), ((), ())),
                                    precision=lax.Precision.HIGHEST, preferred_element_type=F32)
            m_even, m_odd = outer[:32, :128], outer[32:64, :128]
            h_even, h_odd = outer[64:96, 128:], outer[96:, 128:]
            both.append(jnp.concatenate([
                jnp.where(low, m_even, pltpu.roll(m_odd, 64, 1)),
                jnp.where(low, pltpu.roll(m_even, 64, 1), m_odd),
                jnp.where(low, h_even, pltpu.roll(h_odd, 64, 1))], axis=0))
        for k in range(4):
            hsend[k] = jnp.concatenate([both[0][24 * k:24 * k + 24], both[1][24 * k:24 * k + 24]], axis=0).astype(BF16)
        for k in (1, 2, 3):
            made = pltpu.make_async_remote_copy(
                src_ref=hsend.at[blocks[k]], dst_ref=hrecv.at[k - 1], send_sem=h_send.at[k - 1],
                recv_sem=h_recv.at[k - 1], device_id=me.tensor(k), device_id_type=MESH)
            made.start()
            h_copies.append(made)

    def shard():
        g32[pl.ds(pl.multiple_of(48 * t, 48), 48), :] = hsend[t].astype(F32)
        for k in (1, 2, 3):
            h_copies[k - 1].wait_recv()
            g32[pl.ds(pl.multiple_of(48 * ((t + 4 - k) % 4), 48), 48), :] = hrecv[k - 1].astype(F32)
        for k in range(12):
            gpanel[mine, :, 128 * k:128 * k + 128] = jnp.concatenate(
                [g32[pl.ds(k, 8, stride=24), :], g32[pl.ds(k + 12, 8, stride=24), :]], axis=0).astype(BF16)
        sequence = iota((SHARD, 128), 0) % 8
        owner = jnp.zeros((SHARD, 128), F32)
        for j in range(8):
            owner = jnp.where(sequence == j, (slots_ref[j] // 8).astype(F32), owner)
        gpanel[mine, :, HALF:] = owner.astype(BF16)

    n_copies = []

    def new_rows():
        total = jnp.zeros((128, HALF), F32)
        shape = (256, 128)
        right_row = (iota(shape, 0) % SHARD) == iota(shape, 1)
        number = me.dp.astype(F32)
        for i in range(4):
            part = gpanel[pl.ds(16 * i, 16)].reshape(256, PIECE)
            owner = part[:, HALF:].astype(F32)
            pick = jnp.where(jnp.logical_and(right_row, owner == number), 1.0, 0.0).astype(BF16)
            total += lax.dot_general(pick, part[:, :HALF], (((0,), (0,)), ((), ())), preferred_element_type=F32)
        rows = jnp.concatenate([total[:8], total[8:16]], axis=1)
        new_ref[...] = rows.astype(BF16)
        left = jnp.concatenate([rows, rows], axis=0).astype(BF16)
        halves = []
        for c in range(2):
            halves.append(jnp.concatenate(
                [product(left, panel[pl.ds(32 * c + 8 * i, 8)].reshape(128, FEAT))[:8] for i in range(4)], axis=1))
        nsend[...] = jnp.concatenate(halves, axis=0).astype(BF16)
        for k in (1, 2, 3):
            n_copies.append(pltpu.make_async_remote_copy(
                src_ref=nsend, dst_ref=nrecv.at[k - 1], send_sem=n_send.at[k - 1],
                recv_sem=n_recv.at[k - 1], device_id=me.tensor(k), device_id_type=MESH))
        for k in (1, 2, 3):
            @pl.when((t + k) % 4 == 3)
            def _():
                n_copies[k - 1].start()

    def new_scores():
        @pl.when(t == 3)
        def _():
            for made in n_copies:
                made.wait_recv()
            total = nsend[...].astype(F32)
            for k in range(3):
                total += nrecv[k].astype(F32)
            for c in range(2):
                turned = jnp.transpose(jnp.concatenate(
                    [jnp.zeros((120, 512), F32), total[8 * c:8 * c + 8]], axis=0))
                for z in range(2):
                    for b in range(4):
                        for a in range(4):
                            target = pl.ds(pl.multiple_of(me.queries_of(c, z, b, a) * SHARD, SHARD), SHARD)
                            at = slot(0, z, b, a) * SHARD
                            out_ref[target, 128:] += turned[at:at + SHARD]
        for k in (1, 2, 3):
            @pl.when((t + k) % 4 == 3)
            def _():
                n_copies[k - 1].wait_send()

    acc[...] = jnp.zeros_like(acc)
    grads = Gather(me, gpanel, g_send, g_recv)

    def chunk(i):
        gather.wait(*[place for place in CHUNKS[i] if place != (0, 0, 0, 0)])
        stage1(i)

    for made in hidden_in:
        made.wait()
    for made in stored_in:
        made.start()
    factors_part(0, 9)
    gather.on_a(0, 1)
    gather.on_a(0, 3)
    gather.on_z()
    gather.on_b(0, 0)
    factors_part(9, 14)
    factors_send()
    gather.on_a(0, 2)
    for made in stored_in:
        made.wait()
    chunk(0)
    gather.on_b(0, 1)
    gather.pass_on(0, True)
    gather.on_b(0, 3)
    gather.on_a(1, 1)
    gather.on_a(1, 3)
    chunk(1)
    gather.on_b(0, 2)
    gather.pass_on(0, False)
    gather.on_a(1, 2)
    gather.on_b(1, 0)
    chunk(2)
    stage2(0)
    gradients()
    gather.on_b(1, 1)
    gather.pass_on(1, True)
    gather.on_b(1, 3)
    gather.on_opposite(0)
    gather.on_b(1, 2)
    gather.pass_on(1, False)
    stage2(1)
    shard()
    grads.start()
    chunk(3)
    gather.on_opposite(1)
    stage2(2)
    grads.on_a(0, 1)
    grads.on_a(0, 3)
    chunk(4)
    grads.on_a(0, 2)
    grads.on_z()
    grads.on_b(0, 0)
    chunk(5)
    stage3(0)
    grads.on_b(0, 1)
    grads.pass_on(0, True)
    grads.on_b(0, 3)
    grads.on_b(0, 2)
    grads.pass_on(0, False)
    stage2(3)
    grads.on_a(1, 1)
    grads.on_a(1, 3)
    grads.on_a(1, 2)
    grads.on_b(1, 0)
    stage3(1)
    stage2(4)
    grads.on_opposite(0)
    grads.on_b(1, 1)
    grads.pass_on(1, True)
    grads.on_b(1, 3)
    grads.on_b(1, 2)
    grads.pass_on(1, False)
    stage3(2)
    stage2(5)
    stage3(3)
    grads.on_opposite(1)
    grads.wait(*[(p, z, b, a) for p in range(2) for z in range(2) for b in range(4) for a in range(4) if p + z + b + a])
    new_rows()
    stage3(4)
    stage3(5)
    new_scores()

    gather.finish()
    grads.finish()
    for made in rs_copies + fac_copies + h_copies:
        made.wait_send()


def body(acts, gate_pre, up_pre, hidden_cot, out_cot, proj_model, proj_hidden, stored, queries, slots):
    tokens, model = acts.shape
    hidden = gate_pre.shape[1]
    vmem = pltpu.VMEM
    dma = pltpu.SemaphoreType.DMA
    new_block, turned = pl.pallas_call(
        kernel,
        out_shape=(jax.ShapeDtypeStruct((8, FEAT), BF16), jax.ShapeDtypeStruct((NQ, ROWS), F32)),
        in_specs=[pl.BlockSpec(memory_space=pl.ANY)] * 9 + [pl.BlockSpec(memory_space=pltpu.SMEM)],
        out_specs=(pl.BlockSpec(memory_space=pltpu.VMEM), pl.BlockSpec(memory_space=pltpu.VMEM)),
        scratch_shapes=[
            vmem((tokens, model), BF16), vmem((tokens, hidden), BF16), vmem((tokens, hidden), BF16),
            vmem((tokens, hidden), BF16), vmem((tokens, model), BF16), vmem((RANK, model), BF16),
            vmem((RANK, hidden), BF16), vmem((4 * ROWS, FEAT), BF16), vmem((64, SHARD, FEAT), BF16),
            vmem((64, SHARD, PIECE), BF16),
            vmem((384, RANK), F32), vmem((128, FLANES), BF16), vmem((3, 32, FLANES), BF16),
            vmem((4, 48, 128), BF16), vmem((3, 48, 128), BF16), vmem((192, 128), F32),
            vmem((6, NQ, 128), BF16), vmem((6, NQ, 128), BF16),
            vmem((NQ, 128), F32), vmem((NQ, 128), F32), vmem((NQ, ROWS), F32),
            vmem((SHARD, 512), BF16), vmem((3, SHARD, 512), BF16),
            dma((12,)), dma((GATHER_COPIES,)), dma((GATHER_COPIES,)), dma((GATHER_COPIES,)), dma((GATHER_COPIES,)),
            dma((6 * N_CHUNKS,)), dma((6 * N_CHUNKS,)), dma((3,)), dma((3,)), dma((3,)), dma((3,)), dma((3,)), dma((3,)),
        ],
        compiler_params=pltpu.CompilerParams(
            collective_id=0, has_side_effects=True, vmem_limit_bytes=56 * 2**20),
    )(acts, gate_pre, up_pre, hidden_cot, out_cot, proj_model, proj_hidden, stored, queries, slots)
    return new_block, turned.T


def solution(mesh):
    return jax.shard_map(
        body,
        mesh=mesh,
        in_specs=(
            P("dp", "tensor"), P("dp", "tensor"), P("dp", "tensor"), P("dp", "tensor"), P("dp", "tensor"),
            P(None, "tensor"), P(None, "tensor"), P("dp", "tensor"), P("dp", "tensor"), P("dp"),
        ),
        out_specs=(P("dp", "tensor"), P(("dp", "tensor"), None)),
        check_vma=False,
    )
```

```python
import jax
import jax.numpy as jnp
from jax import lax
from jax.experimental import pallas as pl
from jax.experimental.pallas import tpu as pltpu
from jax.sharding import PartitionSpec as P

MESH = pl.DeviceIdType.MESH
BF16, F32 = jnp.bfloat16, jnp.float32
RANK = 64
SHARD = 16
ROWS = 256
NQ = 1024
FEAT = 3072
HALF = FEAT // 2
PIECE = HALF + 128
TILE = 512
FLANES = 384


def product(left, right):
    return lax.dot_general(left, right, (((1,), (1,)), ((), ())), preferred_element_type=F32)


def iota(shape, dim):
    return lax.broadcasted_iota(jnp.int32, shape, dim)


class Place:
    def __init__(self):
        dp = lax.axis_index("dp")
        self.dp, self.t = dp, lax.axis_index("tensor")
        self.core = dp % 2
        self.x, self.y, self.zl = (dp // 2) % 4, (dp // 8) % 4, dp // 32
        self.a = self.x + self.core * (self.y - self.x)
        self.b = self.y + self.core * (self.x - self.y)

    def at(self, a, b, zl):
        x = a + self.core * (b - a)
        y = b + self.core * (a - b)
        return (((zl * 4 + y) * 4 + x) * 2 + self.core, self.t)

    def sibling(self):
        return (self.dp + 1 - 2 * self.core, self.t)

    def z_partner(self):
        return self.at(self.a, self.b, 1 - self.zl)

    def a_peer(self, k):
        return self.at((self.a + k) % 4, self.b, self.zl)

    def b_peer(self, k):
        return self.at(self.a, (self.b + k) % 4, self.zl)

    def tensor(self, k):
        return (self.dp, (self.t + k) % 4)

    def queries_of(self, p, z, b, a):
        core = self.core + p * (1 - 2 * self.core)
        first, second = (self.a, self.b) if p == 0 else (self.b, self.a)
        a_at, b_at, z_at = (first + a) % 4, (second + b) % 4, (self.zl + z) % 2
        x = a_at + core * (b_at - a_at)
        y = b_at + core * (a_at - b_at)
        return ((z_at * 4 + y) * 4 + x) * 2 + core


def slot(p, z, b, a):
    return ((p * 2 + z) * 4 + b) * 4 + a


class Gather:
    def __init__(self, me, panel, send, recv):
        self.me, self.panel, self.send, self.recv = me, panel, send, recv
        self.count = 0
        self.copies, self.landing, self.landed = [], {}, set()

    def copy(self, source, target, device, size=1):
        i = self.count
        self.count += 1
        made = pltpu.make_async_remote_copy(
            src_ref=self.panel.at[pl.ds(slot(*source), size)], dst_ref=self.panel.at[pl.ds(slot(*target), size)],
            send_sem=self.send.at[i], recv_sem=self.recv.at[i], device_id=device, device_id_type=MESH)
        made.start()
        self.copies.append(made)
        for j in range(size):
            self.landing[slot(*target) + j] = i

    def wait(self, *places):
        for place in places:
            i = self.landing[slot(*place)]
            if i not in self.landed:
                self.landed.add(i)
                self.copies[i].wait_recv()

    def to_sibling(self, z, b, a, size=1):
        self.copy((0, z, b, a), (1, z, b, a), self.me.sibling(), size)

    def along_a(self, z, k):
        self.copy((0, z, 0, 0), (0, z, 0, 4 - k), self.me.a_peer(k))

    def along_b(self, z, a):
        for k in (1, 3):
            self.copy((0, z, 0, a), (0, z, 4 - k, a), self.me.b_peer(k))

    def start(self):
        self.to_sibling(0, 0, 0)
        self.along_a(0, 1)
        self.along_a(0, 3)
        self.along_b(0, 0)
        self.copy((0, 0, 0, 0), (0, 1, 0, 0), self.me.z_partner())
        self.along_a(0, 2)

    def on_z(self):
        self.wait((0, 1, 0, 0))
        self.along_a(1, 1)
        self.along_a(1, 3)
        self.along_b(1, 0)
        self.along_a(1, 2)
        self.to_sibling(1, 0, 0)

    def on_a(self, z, a):
        self.wait((0, z, 0, a))
        self.along_b(z, a)
        self.to_sibling(z, 0, a)

    def on_b(self, z, a):
        for b in (1, 3):
            self.wait((0, z, b, a))
            self.to_sibling(z, b, a)

    def pass_on(self, z, low):
        if low:
            self.copy((0, z, 3, 0), (0, z, 2, 0), self.me.b_peer(1), 2)
        else:
            self.copy((0, z, 1, 2), (0, z, 2, 2), self.me.b_peer(3), 2)

    def on_opposite(self, z):
        self.wait((0, z, 2, 0), (0, z, 2, 2))
        self.to_sibling(z, 2, 0, 4)

    def finish(self):
        for made in self.copies:
            made.wait_send()


GATHER_COPIES = 7 + 9 + 6 + 9 + 16 + 4 + 2

CHUNKS = [
    [(0, 0, 0, 0), (1, 0, 0, 0), (0, 0, 0, 1), (0, 0, 0, 3), (1, 0, 0, 1), (1, 0, 0, 3), (0, 0, 1, 0), (0, 0, 3, 0)],
    [(0, 0, 0, 2), (1, 0, 0, 2), (0, 0, 1, 1), (0, 0, 3, 1), (0, 0, 1, 3), (0, 0, 3, 3), (1, 0, 1, 0), (1, 0, 3, 0)],
    [(0, 1, 0, 0), (1, 1, 0, 0), (0, 1, 0, 1), (0, 1, 0, 3), (1, 1, 0, 1), (1, 1, 0, 3), (0, 0, 1, 2), (0, 0, 3, 2)],
    [(1, 0, b, a) for b in (1, 3) for a in (1, 2, 3)] + [(0, 1, 0, 2), (1, 1, 0, 2), (0, 1, 1, 0), (0, 1, 3, 0)],
    [(p, 0, 2, a) for p in (0, 1) for a in range(4)] + [(0, 1, b, a) for b in (1, 3) for a in (1, 2, 3)],
    [(1, 1, b, a) for b in (1, 3) for a in range(4)] + [(p, 1, 2, a) for p in (0, 1) for a in range(4)],
]
CHUNK_ROWS = [SHARD * len(parts) for parts in CHUNKS]
CHUNK_AT = [sum(CHUNK_ROWS[:i]) for i in range(len(CHUNK_ROWS))]
N_CHUNKS = len(CHUNK_ROWS)


def kernel(acts_hbm, gate_hbm, up_hbm, cot_hbm, outc_hbm, pm_hbm, ph_hbm, stored_hbm, queries_hbm, slots_ref,
           new_ref, out_ref,
           acts, gate, up, cot, outc, pm, ph, stored, panel, gpanel,
           acc, chosen, fac, fac_in, hsend, hrecv, g32,
           send, recv, pp, pm_part, po, nsend, nrecv,
           local_sem, q_send, q_recv, g_send, g_recv, rs_send, rs_recv, f_send, f_recv, h_send, h_recv, n_send, n_recv):
    me = Place()
    t = me.t

    mine = 0
    own_q = pltpu.make_async_copy(queries_hbm, panel.at[mine], local_sem.at[0])
    own_q.start()
    stored_in = [
        pltpu.make_async_copy(stored_hbm.at[pl.ds(256 * i, 256 if i < 3 else 248)],
                              stored.at[pl.ds(256 * i, 256 if i < 3 else 248)], local_sem.at[1 + i])
        for i in range(4)
    ]
    stored[1008:, :] = jnp.zeros((16, FEAT), BF16)
    hidden_in = [pltpu.make_async_copy(src, dst, local_sem.at[5 + i]) for i, (src, dst) in enumerate(
        [(gate_hbm, gate), (up_hbm, up), (cot_hbm, cot), (ph_hbm, ph), (acts_hbm, acts), (outc_hbm, outc), (pm_hbm, pm)])]

    for made in hidden_in:
        made.start()

    barrier = pltpu.get_barrier_semaphore()
    partners = [me.sibling(), me.z_partner()]
    for k in (1, 2, 3):
        partners += [me.a_peer(k), me.b_peer(k), me.tensor(k)]
    for device in partners:
        pl.semaphore_signal(barrier, inc=1, device_id=device, device_id_type=MESH)
    pl.semaphore_wait(barrier, len(partners))

    gather = Gather(me, panel, q_send, q_recv)
    own_q.wait()
    gather.start()

    blocks = [(t + k) % 4 for k in range(4)]
    rs_copies = []

    def rs_copy(i, kind, k):
        rows = pl.ds(CHUNK_AT[i], CHUNK_ROWS[i])
        made = pltpu.make_async_remote_copy(
            src_ref=send.at[kind, rows], dst_ref=recv.at[kind, rows], send_sem=rs_send.at[6 * i + kind],
            recv_sem=rs_recv.at[6 * i + kind], device_id=me.tensor(k), device_id_type=MESH)
        made.start()
        rs_copies.append(made)
        reduce[i, kind] = made

    def score(i, block):
        total = None
        for column in range(0, FEAT, TILE):
            left = jnp.concatenate(
                [panel[slot(*place), :, column:column + TILE] for place in CHUNKS[i]], axis=0)
            right = stored[pl.ds(pl.multiple_of(block * ROWS, ROWS), ROWS), column:column + TILE]
            term = product(left, right)
            total = term if total is None else total + term
        return total

    reduce = {}

    def stage1(i):
        rows = pl.ds(CHUNK_AT[i], CHUNK_ROWS[i])
        part = score(i, blocks[2])
        send[0, rows, :] = part[:, :128].astype(BF16)
        rs_copy(i, 0, 1)
        send[1, rows, :] = part[:, 128:].astype(BF16)
        rs_copy(i, 1, 3)
        part = score(i, blocks[1])
        send[2, rows, :] = part[:, 128:].astype(BF16)
        rs_copy(i, 2, 1)
        pp[rows, :] = part[:, :128]
        part = score(i, blocks[3])
        send[3, rows, :] = part[:, :128].astype(BF16)
        rs_copy(i, 3, 3)
        pm_part[rows, :] = part[:, 128:]
        po[rows, :] = score(i, blocks[0])

    def stage2(i):
        rows = pl.ds(CHUNK_AT[i], CHUNK_ROWS[i])
        reduce[i, 0].wait_recv()
        send[4, rows, :] = (pp[rows, :] + recv[0, rows, :].astype(F32)).astype(BF16)
        rs_copy(i, 4, 1)
        reduce[i, 1].wait_recv()
        send[5, rows, :] = (pm_part[rows, :] + recv[1, rows, :].astype(F32)).astype(BF16)
        rs_copy(i, 5, 3)

    def stage3(i):
        for kind in (2, 3, 4, 5):
            reduce[i, kind].wait_recv()
        for j, place in enumerate(CHUNKS[i]):
            rows = pl.ds(CHUNK_AT[i] + SHARD * j, SHARD)
            target = pl.ds(pl.multiple_of(me.queries_of(*place) * SHARD, SHARD), SHARD)
            out_ref[target, :128] = po[rows, :128] + recv[3, rows, :].astype(F32) + recv[4, rows, :].astype(F32)
            out_ref[target, 128:] = po[rows, 128:] + recv[2, rows, :].astype(F32) + recv[5, rows, :].astype(F32)

    def factors_part(begin, end):
        def step(i, total):
            columns = pl.ds(pl.multiple_of(i * TILE, TILE), TILE)
            g = gate[:, columns].astype(F32)
            u = up[:, columns].astype(F32)
            c = cot[:, columns].astype(F32)
            s = 0.5 * jnp.tanh(0.5 * g) + 0.5
            silu = g * s
            hidden = (silu * u).astype(BF16)
            up_cot = (c * silu).astype(BF16)
            gate_cot = (c * u * (s + silu * (1.0 - s))).astype(BF16)
            return total + product(jnp.concatenate([gate_cot, up_cot, hidden], axis=0), ph[:, columns])

        acc[...] += lax.fori_loop(begin, end, step, jnp.zeros((384, RANK), F32))

    fac_copies, h_copies = {}, {}

    def factors_send():
        model = product(jnp.concatenate([acts[...], outc[...]], axis=0), pm[...]).astype(BF16)
        hidden = acc[...].astype(BF16)
        row, lane = iota((RANK, FLANES), 0), iota((RANK, FLANES), 1)
        split = (row % 2) * 32 + row // 2

        def spread(value, target):
            return jnp.dot(value, (lane == target).astype(F32).astype(BF16), preferred_element_type=F32)

        fac[...] = (spread(model[:128], split) + spread(hidden[256:], split + 64) + spread(hidden[:128], row + 128)
                    + spread(hidden[128:256], row + 192) + spread(model[128:], row + 256)).astype(BF16)
        for k in (2, 1, 3):
            made = pltpu.make_async_remote_copy(
                src_ref=fac.at[pl.ds(pl.multiple_of(32 * blocks[k], 32), 32)], dst_ref=fac_in.at[k - 1],
                send_sem=f_send.at[k - 1], recv_sem=f_recv.at[k - 1],
                device_id=me.tensor(k), device_id_type=MESH)
            made.start()
            fac_copies[k] = made

    def gradients():
        total = fac[pl.ds(pl.multiple_of(32 * t, 32), 32), :].astype(F32)
        for k in (1, 2, 3):
            fac_copies[k].wait_recv()
            total += fac_in[k - 1].astype(F32)
        low = iota((32, 128), 1) < RANK
        both = []
        for s in range(2):
            one = total[16 * s:16 * s + 16]
            outer = lax.dot_general(one[:, :128], one[:, 128:], (((0,), (0,)), ((), ())),
                                    precision=lax.Precision.HIGHEST, preferred_element_type=F32)
            m_even, m_odd = outer[:32, :128], outer[32:64, :128]
            h_even, h_odd = outer[64:96, 128:], outer[96:, 128:]
            both.append(jnp.concatenate([
                jnp.where(low, m_even, pltpu.roll(m_odd, 64, 1)),
                jnp.where(low, pltpu.roll(m_even, 64, 1), m_odd),
                jnp.where(low, h_even, pltpu.roll(h_odd, 64, 1))], axis=0))
        for k in range(4):
            hsend[k] = jnp.concatenate([both[0][24 * k:24 * k + 24], both[1][24 * k:24 * k + 24]], axis=0).astype(BF16)
        for k in (2, 1, 3):
            made = pltpu.make_async_remote_copy(
                src_ref=hsend.at[blocks[k]], dst_ref=hrecv.at[k - 1], send_sem=h_send.at[k - 1],
                recv_sem=h_recv.at[k - 1], device_id=me.tensor(k), device_id_type=MESH)
            made.start()
            h_copies[k] = made

    def shard():
        g32[pl.ds(pl.multiple_of(48 * t, 48), 48), :] = hsend[t].astype(F32)
        for k in (1, 2, 3):
            h_copies[k].wait_recv()
            g32[pl.ds(pl.multiple_of(48 * ((t + 4 - k) % 4), 48), 48), :] = hrecv[k - 1].astype(F32)
        for k in range(12):
            gpanel[mine, :, 128 * k:128 * k + 128] = jnp.concatenate(
                [g32[pl.ds(k, 8, stride=24), :], g32[pl.ds(k + 12, 8, stride=24), :]], axis=0).astype(BF16)
        sequence = iota((SHARD, 128), 0) % 8
        owner = jnp.zeros((SHARD, 128), F32)
        for j in range(8):
            owner = jnp.where(sequence == j, (slots_ref[j] // 8).astype(F32), owner)
        gpanel[mine, :, HALF:] = owner.astype(BF16)

    n_copies = []

    def pick(part):
        shape = (256, 128)
        right_row = (iota(shape, 0) % SHARD) == iota(shape, 1)
        owner = part[:, HALF:].astype(F32)
        chosen = jnp.where(jnp.logical_and(right_row, owner == me.dp.astype(F32)), 1.0, 0.0).astype(BF16)
        return lax.dot_general(chosen, part[:, :HALF], (((0,), (0,)), ((), ())), preferred_element_type=F32)[:SHARD]

    def picked(z):
        grads.wait(*[(p, z, b, a) for p in range(2) for b in range(4) for a in range(4) if p + z + b + a])
        chosen[...] += pick(gpanel[pl.ds(slot(0, z, 0, 0), 16)].reshape(256, PIECE))
        chosen[...] += pick(gpanel[pl.ds(slot(1, z, 0, 0), 16)].reshape(256, PIECE))

    def new_rows():
        total = chosen[...]
        rows = jnp.concatenate([total[:8], total[8:16]], axis=1)
        new_ref[...] = rows.astype(BF16)
        left = jnp.concatenate([rows, rows], axis=0).astype(BF16)
        halves = []
        for c in range(2):
            halves.append(jnp.concatenate(
                [product(left, panel[pl.ds(32 * c + 8 * i, 8)].reshape(128, FEAT))[:8] for i in range(4)], axis=1))
        nsend[...] = jnp.concatenate(halves, axis=0).astype(BF16)
        for k in (1, 2, 3):
            n_copies.append(pltpu.make_async_remote_copy(
                src_ref=nsend, dst_ref=nrecv.at[k - 1], send_sem=n_send.at[k - 1],
                recv_sem=n_recv.at[k - 1], device_id=me.tensor(k), device_id_type=MESH))
        for k in (1, 2, 3):
            @pl.when((t + k) % 4 == 3)
            def _():
                n_copies[k - 1].start()

    def new_scores():
        @pl.when(t == 3)
        def _():
            for made in n_copies:
                made.wait_recv()
            total = nsend[...].astype(F32)
            for k in range(3):
                total += nrecv[k].astype(F32)
            for c in range(2):
                turned = jnp.transpose(jnp.concatenate(
                    [jnp.zeros((120, 512), F32), total[8 * c:8 * c + 8]], axis=0))
                for i, parts in enumerate(CHUNKS):
                    for j, place in enumerate(parts):
                        if place[0] == c:
                            at = slot(0, *place[1:]) * SHARD
                            po[pl.ds(CHUNK_AT[i] + SHARD * j, SHARD), 128:] += turned[at:at + SHARD]
        for k in (1, 2, 3):
            @pl.when((t + k) % 4 == 3)
            def _():
                n_copies[k - 1].wait_send()

    acc[...] = jnp.zeros_like(acc)
    chosen[...] = jnp.zeros_like(chosen)
    grads = Gather(me, gpanel, g_send, g_recv)

    def chunk(i):
        gather.wait(*[place for place in CHUNKS[i] if place != (0, 0, 0, 0)])
        stage1(i)

    for made in hidden_in:
        made.wait()
    for made in stored_in:
        made.start()
    factors_part(0, 14)
    gather.on_a(0, 1)
    gather.on_a(0, 3)
    factors_send()
    gather.on_z()
    gather.on_b(0, 0)
    for made in stored_in:
        made.wait()
    chunk(0)
    gather.on_a(0, 2)
    gather.on_b(0, 1)
    gather.pass_on(0, True)
    gather.on_b(0, 3)
    gather.on_a(1, 1)
    gather.on_a(1, 3)
    chunk(1)
    gradients()
    gather.on_b(0, 2)
    gather.pass_on(0, False)
    gather.on_a(1, 2)
    gather.on_b(1, 0)
    stage2(0)
    chunk(2)
    gather.on_b(1, 1)
    gather.pass_on(1, True)
    gather.on_b(1, 3)
    gather.on_opposite(0)
    gather.on_b(1, 2)
    gather.pass_on(1, False)
    stage2(1)
    shard()
    grads.start()
    chunk(3)
    gather.on_opposite(1)
    grads.on_a(0, 1)
    grads.on_a(0, 3)
    grads.on_z()
    grads.on_a(0, 2)
    grads.on_b(0, 0)
    stage2(2)
    chunk(4)
    grads.on_b(0, 1)
    grads.pass_on(0, True)
    grads.on_b(0, 3)
    grads.on_a(1, 1)
    grads.on_a(1, 3)
    grads.on_a(1, 2)
    grads.on_b(0, 2)
    grads.pass_on(0, False)
    grads.on_b(1, 0)
    chunk(5)
    grads.on_b(1, 1)
    grads.pass_on(1, True)
    grads.on_b(1, 3)
    grads.on_b(1, 2)
    grads.pass_on(1, False)
    stage2(3)
    grads.on_opposite(0)
    stage2(4)
    picked(0)
    stage2(5)
    grads.on_opposite(1)
    picked(1)
    new_rows()
    new_scores()
    for i in range(N_CHUNKS):
        stage3(i)


    gather.finish()
    grads.finish()
    for made in rs_copies + list(fac_copies.values()) + list(h_copies.values()):
        made.wait_send()


def finish(rows_ref, turned_ref, new_ref, scores_ref):
    new_ref[...] = rows_ref[...]
    scores_ref[...] = turned_ref[...].T


def body(acts, gate_pre, up_pre, hidden_cot, out_cot, proj_model, proj_hidden, stored, queries, slots):
    tokens, model = acts.shape
    hidden = gate_pre.shape[1]
    vmem = pltpu.VMEM
    dma = pltpu.SemaphoreType.DMA
    new_block, turned = pl.pallas_call(
        kernel,
        out_shape=(jax.ShapeDtypeStruct((8, FEAT), BF16), jax.ShapeDtypeStruct((NQ, ROWS), F32)),
        in_specs=[pl.BlockSpec(memory_space=pl.ANY)] * 9 + [pl.BlockSpec(memory_space=pltpu.SMEM)],
        out_specs=(pl.BlockSpec(memory_space=pltpu.VMEM), pl.BlockSpec(memory_space=pltpu.VMEM)),
        scratch_shapes=[
            vmem((tokens, model), BF16), vmem((tokens, hidden), BF16), vmem((tokens, hidden), BF16),
            vmem((tokens, hidden), BF16), vmem((tokens, model), BF16), vmem((RANK, model), BF16),
            vmem((RANK, hidden), BF16), vmem((4 * ROWS, FEAT), BF16), vmem((64, SHARD, FEAT), BF16),
            vmem((64, SHARD, PIECE), BF16),
            vmem((384, RANK), F32), vmem((SHARD, HALF), F32), vmem((128, FLANES), BF16), vmem((3, 32, FLANES), BF16),
            vmem((4, 48, 128), BF16), vmem((3, 48, 128), BF16), vmem((192, 128), F32),
            vmem((6, NQ, 128), BF16), vmem((6, NQ, 128), BF16),
            vmem((NQ, 128), F32), vmem((NQ, 128), F32), vmem((NQ, ROWS), F32),
            vmem((SHARD, 512), BF16), vmem((3, SHARD, 512), BF16),
            dma((12,)), dma((GATHER_COPIES,)), dma((GATHER_COPIES,)), dma((GATHER_COPIES,)), dma((GATHER_COPIES,)),
            dma((6 * N_CHUNKS,)), dma((6 * N_CHUNKS,)), dma((3,)), dma((3,)), dma((3,)), dma((3,)), dma((3,)), dma((3,)),
        ],
        compiler_params=pltpu.CompilerParams(
            collective_id=0, has_side_effects=True, vmem_limit_bytes=56 * 2**20),
    )(acts, gate_pre, up_pre, hidden_cot, out_cot, proj_model, proj_hidden, stored, queries, slots)
    return pl.pallas_call(
        finish,
        out_shape=(jax.ShapeDtypeStruct((8, FEAT), BF16), jax.ShapeDtypeStruct((ROWS, NQ), F32)),
    )(new_block, turned)


def solution(mesh):
    return jax.shard_map(
        body,
        mesh=mesh,
        in_specs=(
            P("dp", "tensor"), P("dp", "tensor"), P("dp", "tensor"), P("dp", "tensor"), P("dp", "tensor"),
            P(None, "tensor"), P(None, "tensor"), P("dp", "tensor"), P("dp", "tensor"), P("dp"),
        ),
        out_specs=(P("dp", "tensor"), P(("dp", "tensor"), None)),
        check_vma=False,
    )
```

```python
import jax
import jax.numpy as jnp
from jax import lax
from jax.experimental import pallas as pl
from jax.experimental.pallas import tpu as pltpu
from jax.sharding import PartitionSpec as P

MESH = pl.DeviceIdType.MESH
BF16, F32 = jnp.bfloat16, jnp.float32
RANK = 64
SHARD = 16
ROWS = 256
NQ = 1024
FEAT = 3072
HALF = FEAT // 2
PIECE = HALF + 128
TILE = 512
FLANES = 384


def product(left, right):
    return lax.dot_general(left, right, (((1,), (1,)), ((), ())), preferred_element_type=F32)


def iota(shape, dim):
    return lax.broadcasted_iota(jnp.int32, shape, dim)


class Place:
    def __init__(self):
        dp = lax.axis_index("dp")
        self.dp, self.t = dp, lax.axis_index("tensor")
        self.core = dp % 2
        self.x, self.y, self.zl = (dp // 2) % 4, (dp // 8) % 4, dp // 32
        self.a = self.x + self.core * (self.y - self.x)
        self.b = self.y + self.core * (self.x - self.y)

    def at(self, a, b, zl):
        x = a + self.core * (b - a)
        y = b + self.core * (a - b)
        return (((zl * 4 + y) * 4 + x) * 2 + self.core, self.t)

    def sibling(self):
        return (self.dp + 1 - 2 * self.core, self.t)

    def z_partner(self):
        return self.at(self.a, self.b, 1 - self.zl)

    def a_peer(self, k):
        return self.at((self.a + k) % 4, self.b, self.zl)

    def b_peer(self, k):
        return self.at(self.a, (self.b + k) % 4, self.zl)

    def tensor(self, k):
        return (self.dp, (self.t + k) % 4)

    def queries_of(self, p, z, b, a):
        core = self.core + p * (1 - 2 * self.core)
        first, second = (self.a, self.b) if p == 0 else (self.b, self.a)
        a_at, b_at, z_at = (first + a) % 4, (second + b) % 4, (self.zl + z) % 2
        x = a_at + core * (b_at - a_at)
        y = b_at + core * (a_at - b_at)
        return ((z_at * 4 + y) * 4 + x) * 2 + core


def slot(p, z, b, a):
    return ((p * 2 + z) * 4 + b) * 4 + a


class Gather:
    def __init__(self, me, panel, send, recv):
        self.me, self.panel, self.send, self.recv = me, panel, send, recv
        self.count = 0
        self.copies, self.landing, self.landed = [], {}, set()

    def copy(self, source, target, device, size=1):
        i = self.count
        self.count += 1
        made = pltpu.make_async_remote_copy(
            src_ref=self.panel.at[pl.ds(slot(*source), size)], dst_ref=self.panel.at[pl.ds(slot(*target), size)],
            send_sem=self.send.at[i], recv_sem=self.recv.at[i], device_id=device, device_id_type=MESH)
        made.start()
        self.copies.append(made)
        for j in range(size):
            self.landing[slot(*target) + j] = i

    def wait(self, *places):
        for place in places:
            i = self.landing[slot(*place)]
            if i not in self.landed:
                self.landed.add(i)
                self.copies[i].wait_recv()

    def to_sibling(self, z, b, a, size=1):
        self.copy((0, z, b, a), (1, z, b, a), self.me.sibling(), size)

    def along_a(self, z, k):
        self.copy((0, z, 0, 0), (0, z, 0, 4 - k), self.me.a_peer(k))

    def along_b(self, z, a):
        for k in (1, 3):
            self.copy((0, z, 0, a), (0, z, 4 - k, a), self.me.b_peer(k))

    def start(self):
        self.to_sibling(0, 0, 0)
        self.along_a(0, 1)
        self.along_a(0, 3)
        self.along_b(0, 0)
        self.copy((0, 0, 0, 0), (0, 1, 0, 0), self.me.z_partner())
        self.along_a(0, 2)

    def on_z(self):
        self.wait((0, 1, 0, 0))
        self.along_a(1, 1)
        self.along_a(1, 3)
        self.along_b(1, 0)
        self.along_a(1, 2)
        self.to_sibling(1, 0, 0)

    def on_a(self, z, a):
        self.wait((0, z, 0, a))
        self.along_b(z, a)
        self.to_sibling(z, 0, a)

    def on_b(self, z, a):
        for b in (1, 3):
            self.wait((0, z, b, a))
            self.to_sibling(z, b, a)

    def pass_on(self, z, low):
        if low:
            self.copy((0, z, 3, 0), (0, z, 2, 0), self.me.b_peer(1), 2)
        else:
            self.copy((0, z, 1, 2), (0, z, 2, 2), self.me.b_peer(3), 2)

    def on_opposite(self, z):
        self.wait((0, z, 2, 0), (0, z, 2, 2))
        self.to_sibling(z, 2, 0, 4)

    def finish(self):
        for made in self.copies:
            made.wait_send()


GATHER_COPIES = 7 + 9 + 6 + 9 + 16 + 4 + 2

CHUNKS = [
    [(0, 0, 0, 0), (1, 0, 0, 0), (0, 0, 0, 1), (0, 0, 0, 3), (1, 0, 0, 1), (1, 0, 0, 3), (0, 0, 1, 0), (0, 0, 3, 0)],
    [(0, 0, 0, 2), (1, 0, 0, 2), (0, 0, 1, 1), (0, 0, 3, 1), (0, 0, 1, 3), (0, 0, 3, 3), (1, 0, 1, 0), (1, 0, 3, 0)],
    [(0, 1, 0, 0), (1, 1, 0, 0), (0, 1, 0, 1), (0, 1, 0, 3), (1, 1, 0, 1), (1, 1, 0, 3), (0, 0, 1, 2), (0, 0, 3, 2)],
    [(1, 0, b, a) for b in (1, 3) for a in (1, 2, 3)] + [(0, 1, 0, 2), (1, 1, 0, 2), (0, 1, 1, 0), (0, 1, 3, 0)],
    [(p, 0, 2, a) for p in (0, 1) for a in range(4)] + [(0, 1, b, a) for b in (1, 3) for a in (1, 2, 3)],
    [(1, 1, b, a) for b in (1, 3) for a in range(4)] + [(p, 1, 2, a) for p in (0, 1) for a in range(4)],
]
CHUNK_ROWS = [SHARD * len(parts) for parts in CHUNKS]
CHUNK_AT = [sum(CHUNK_ROWS[:i]) for i in range(len(CHUNK_ROWS))]
N_CHUNKS = len(CHUNK_ROWS)


def kernel(acts_hbm, gate_hbm, up_hbm, cot_hbm, outc_hbm, pm_hbm, ph_hbm, stored_hbm, queries_hbm, slots_ref,
           new_ref, out_ref,
           acts, gate, up, cot, outc, pm, ph, stored, panel, gpanel,
           acc, chosen, fac, fac_in, hsend, hrecv, g32,
           send, recv, pp, pm_part, po, nsend, nrecv,
           local_sem, q_send, q_recv, g_send, g_recv, rs_send, rs_recv, f_send, f_recv, h_send, h_recv, n_send, n_recv):
    me = Place()
    t = me.t

    mine = 0
    own_q = pltpu.make_async_copy(queries_hbm, panel.at[mine], local_sem.at[0])
    own_q.start()
    stored_in = [
        pltpu.make_async_copy(stored_hbm.at[pl.ds(256 * i, 256 if i < 3 else 248)],
                              stored.at[pl.ds(256 * i, 256 if i < 3 else 248)], local_sem.at[1 + i])
        for i in range(4)
    ]
    stored[1008:, :] = jnp.zeros((16, FEAT), BF16)
    hidden_in = [pltpu.make_async_copy(src, dst, local_sem.at[5 + i]) for i, (src, dst) in enumerate(
        [(gate_hbm, gate), (up_hbm, up), (cot_hbm, cot), (ph_hbm, ph), (acts_hbm, acts), (outc_hbm, outc), (pm_hbm, pm)])]

    for made in hidden_in:
        made.start()

    barrier = pltpu.get_barrier_semaphore()
    partners = [me.sibling(), me.z_partner()]
    for k in (1, 2, 3):
        partners += [me.a_peer(k), me.b_peer(k), me.tensor(k)]
    for device in partners:
        pl.semaphore_signal(barrier, inc=1, device_id=device, device_id_type=MESH)
    pl.semaphore_wait(barrier, len(partners))

    gather = Gather(me, panel, q_send, q_recv)
    own_q.wait()
    gather.start()

    blocks = [(t + k) % 4 for k in range(4)]
    rs_copies = []

    def rs_copy(i, kind, k):
        rows = pl.ds(CHUNK_AT[i], CHUNK_ROWS[i])
        made = pltpu.make_async_remote_copy(
            src_ref=send.at[kind, rows], dst_ref=recv.at[kind, rows], send_sem=rs_send.at[6 * i + kind],
            recv_sem=rs_recv.at[6 * i + kind], device_id=me.tensor(k), device_id_type=MESH)
        made.start()
        rs_copies.append(made)
        reduce[i, kind] = made

    def score(i, block):
        total = None
        for column in range(0, FEAT, TILE):
            left = jnp.concatenate(
                [panel[slot(*place), :, column:column + TILE] for place in CHUNKS[i]], axis=0)
            right = stored[pl.ds(pl.multiple_of(block * ROWS, ROWS), ROWS), column:column + TILE]
            term = product(left, right)
            total = term if total is None else total + term
        return total

    reduce = {}

    def stage1(i):
        rows = pl.ds(CHUNK_AT[i], CHUNK_ROWS[i])
        part = score(i, blocks[2])
        send[0, rows, :] = part[:, :128].astype(BF16)
        rs_copy(i, 0, 1)
        send[1, rows, :] = part[:, 128:].astype(BF16)
        rs_copy(i, 1, 3)
        part = score(i, blocks[1])
        send[2, rows, :] = part[:, 128:].astype(BF16)
        rs_copy(i, 2, 1)
        pp[rows, :] = part[:, :128]
        part = score(i, blocks[3])
        send[3, rows, :] = part[:, :128].astype(BF16)
        rs_copy(i, 3, 3)
        pm_part[rows, :] = part[:, 128:]
        po[rows, :] = score(i, blocks[0])

    def stage2(i):
        rows = pl.ds(CHUNK_AT[i], CHUNK_ROWS[i])
        reduce[i, 0].wait_recv()
        send[4, rows, :] = (pp[rows, :] + recv[0, rows, :].astype(F32)).astype(BF16)
        rs_copy(i, 4, 1)
        reduce[i, 1].wait_recv()
        send[5, rows, :] = (pm_part[rows, :] + recv[1, rows, :].astype(F32)).astype(BF16)
        rs_copy(i, 5, 3)

    def stage3(i):
        for kind in (2, 3, 4, 5):
            reduce[i, kind].wait_recv()
        for j, place in enumerate(CHUNKS[i]):
            rows = pl.ds(CHUNK_AT[i] + SHARD * j, SHARD)
            target = pl.ds(pl.multiple_of(me.queries_of(*place) * SHARD, SHARD), SHARD)
            out_ref[target, :128] = po[rows, :128] + recv[3, rows, :].astype(F32) + recv[4, rows, :].astype(F32)
            out_ref[target, 128:] = po[rows, 128:] + recv[2, rows, :].astype(F32) + recv[5, rows, :].astype(F32)

    def factors_part(begin, end):
        def step(i, total):
            columns = pl.ds(pl.multiple_of(i * TILE, TILE), TILE)
            g = gate[:, columns].astype(F32)
            u = up[:, columns].astype(F32)
            c = cot[:, columns].astype(F32)
            s = 0.5 * jnp.tanh(0.5 * g) + 0.5
            silu = g * s
            hidden = (silu * u).astype(BF16)
            up_cot = (c * silu).astype(BF16)
            gate_cot = (c * u * (s + silu * (1.0 - s))).astype(BF16)
            return total + product(jnp.concatenate([gate_cot, up_cot, hidden], axis=0), ph[:, columns])

        acc[...] += lax.fori_loop(begin, end, step, jnp.zeros((384, RANK), F32))

    fac_copies, h_copies = {}, {}

    def factors_send():
        model = product(jnp.concatenate([acts[...], outc[...]], axis=0), pm[...]).astype(BF16)
        hidden = acc[...].astype(BF16)
        row, lane = iota((RANK, FLANES), 0), iota((RANK, FLANES), 1)
        split = (row % 2) * 32 + row // 2

        def spread(value, target):
            return jnp.dot(value, (lane == target).astype(F32).astype(BF16), preferred_element_type=F32)

        fac[...] = (spread(model[:128], split) + spread(hidden[256:], split + 64) + spread(hidden[:128], row + 128)
                    + spread(hidden[128:256], row + 192) + spread(model[128:], row + 256)).astype(BF16)
        for k in (2, 1, 3):
            made = pltpu.make_async_remote_copy(
                src_ref=fac.at[pl.ds(pl.multiple_of(32 * blocks[k], 32), 32)], dst_ref=fac_in.at[k - 1],
                send_sem=f_send.at[k - 1], recv_sem=f_recv.at[k - 1],
                device_id=me.tensor(k), device_id_type=MESH)
            made.start()
            fac_copies[k] = made

    def gradients():
        total = fac[pl.ds(pl.multiple_of(32 * t, 32), 32), :].astype(F32)
        for k in (1, 2, 3):
            fac_copies[k].wait_recv()
            total += fac_in[k - 1].astype(F32)
        low = iota((32, 128), 1) < RANK
        both = []
        for s in range(2):
            one = total[16 * s:16 * s + 16]
            outer = lax.dot_general(one[:, :128], one[:, 128:], (((0,), (0,)), ((), ())),
                                    precision=lax.Precision.HIGHEST, preferred_element_type=F32)
            m_even, m_odd = outer[:32, :128], outer[32:64, :128]
            h_even, h_odd = outer[64:96, 128:], outer[96:, 128:]
            both.append(jnp.concatenate([
                jnp.where(low, m_even, pltpu.roll(m_odd, 64, 1)),
                jnp.where(low, pltpu.roll(m_even, 64, 1), m_odd),
                jnp.where(low, h_even, pltpu.roll(h_odd, 64, 1))], axis=0))
        for k in range(4):
            hsend[k] = jnp.concatenate([both[0][24 * k:24 * k + 24], both[1][24 * k:24 * k + 24]], axis=0).astype(BF16)
        for k in (2, 1, 3):
            made = pltpu.make_async_remote_copy(
                src_ref=hsend.at[blocks[k]], dst_ref=hrecv.at[k - 1], send_sem=h_send.at[k - 1],
                recv_sem=h_recv.at[k - 1], device_id=me.tensor(k), device_id_type=MESH)
            made.start()
            h_copies[k] = made

    def shard():
        g32[pl.ds(pl.multiple_of(48 * t, 48), 48), :] = hsend[t].astype(F32)
        for k in (1, 2, 3):
            h_copies[k].wait_recv()
            g32[pl.ds(pl.multiple_of(48 * ((t + 4 - k) % 4), 48), 48), :] = hrecv[k - 1].astype(F32)
        for k in range(12):
            gpanel[mine, :, 128 * k:128 * k + 128] = jnp.concatenate(
                [g32[pl.ds(k, 8, stride=24), :], g32[pl.ds(k + 12, 8, stride=24), :]], axis=0).astype(BF16)
        sequence = iota((SHARD, 128), 0) % 8
        owner = jnp.zeros((SHARD, 128), F32)
        for j in range(8):
            owner = jnp.where(sequence == j, (slots_ref[j] // 8).astype(F32), owner)
        gpanel[mine, :, HALF:] = owner.astype(BF16)

    n_copies = []

    def pick(part):
        shape = (256, 128)
        right_row = (iota(shape, 0) % SHARD) == iota(shape, 1)
        owner = part[:, HALF:].astype(F32)
        chosen = jnp.where(jnp.logical_and(right_row, owner == me.dp.astype(F32)), 1.0, 0.0).astype(BF16)
        return lax.dot_general(chosen, part[:, :HALF], (((0,), (0,)), ((), ())), preferred_element_type=F32)[:SHARD]

    def picked(z):
        grads.wait(*[(p, z, b, a) for p in range(2) for b in range(4) for a in range(4) if p + z + b + a])
        chosen[...] += pick(gpanel[pl.ds(slot(0, z, 0, 0), 16)].reshape(256, PIECE))
        chosen[...] += pick(gpanel[pl.ds(slot(1, z, 0, 0), 16)].reshape(256, PIECE))

    def new_rows():
        total = chosen[...]
        rows = jnp.concatenate([total[:8], total[8:16]], axis=1)
        new_ref[...] = rows.astype(BF16)
        left = jnp.concatenate([rows, rows], axis=0).astype(BF16)
        halves = []
        for c in range(2):
            halves.append(jnp.concatenate(
                [product(left, panel[pl.ds(32 * c + 8 * i, 8)].reshape(128, FEAT))[:8] for i in range(4)], axis=1))
        nsend[...] = jnp.concatenate(halves, axis=0).astype(BF16)
        for k in (1, 2, 3):
            n_copies.append(pltpu.make_async_remote_copy(
                src_ref=nsend, dst_ref=nrecv.at[k - 1], send_sem=n_send.at[k - 1],
                recv_sem=n_recv.at[k - 1], device_id=me.tensor(k), device_id_type=MESH))
        for k in (1, 2, 3):
            @pl.when((t + k) % 4 == 3)
            def _():
                n_copies[k - 1].start()

    def new_scores():
        @pl.when(t == 3)
        def _():
            for made in n_copies:
                made.wait_recv()
            total = nsend[...].astype(F32)
            for k in range(3):
                total += nrecv[k].astype(F32)
            for c in range(2):
                turned = jnp.transpose(jnp.concatenate(
                    [jnp.zeros((120, 512), F32), total[8 * c:8 * c + 8]], axis=0))
                for i, parts in enumerate(CHUNKS):
                    for j, place in enumerate(parts):
                        if place[0] == c:
                            at = slot(0, *place[1:]) * SHARD
                            po[pl.ds(CHUNK_AT[i] + SHARD * j, SHARD), 128:] += turned[at:at + SHARD]
        for k in (1, 2, 3):
            @pl.when((t + k) % 4 == 3)
            def _():
                n_copies[k - 1].wait_send()

    acc[...] = jnp.zeros_like(acc)
    chosen[...] = jnp.zeros_like(chosen)
    grads = Gather(me, gpanel, g_send, g_recv)

    def chunk(i):
        gather.wait(*[place for place in CHUNKS[i] if place != (0, 0, 0, 0)])
        stage1(i)

    for made in hidden_in:
        made.wait()
    for made in stored_in:
        made.start()
    factors_part(0, 14)
    gather.on_a(0, 1)
    gather.on_a(0, 3)
    factors_send()
    gather.on_z()
    gather.on_b(0, 0)
    for made in stored_in:
        made.wait()
    chunk(0)
    gather.on_a(0, 2)
    gather.on_b(0, 1)
    gather.pass_on(0, True)
    gather.on_b(0, 3)
    gather.on_a(1, 1)
    gather.on_a(1, 3)
    chunk(1)
    gradients()
    gather.on_b(0, 2)
    gather.pass_on(0, False)
    gather.on_a(1, 2)
    gather.on_b(1, 0)
    stage2(0)
    chunk(2)
    gather.on_b(1, 1)
    gather.pass_on(1, True)
    gather.on_b(1, 3)
    gather.on_opposite(0)
    gather.on_b(1, 2)
    gather.pass_on(1, False)
    shard()
    grads.start()
    stage2(1)
    chunk(3)
    gather.on_opposite(1)
    grads.on_a(0, 1)
    grads.on_a(0, 3)
    grads.on_z()
    grads.on_a(0, 2)
    grads.on_b(0, 0)
    stage2(2)
    chunk(4)
    grads.on_b(0, 1)
    grads.pass_on(0, True)
    grads.on_b(0, 3)
    grads.on_a(1, 1)
    grads.on_a(1, 3)
    grads.on_a(1, 2)
    grads.on_b(0, 2)
    grads.pass_on(0, False)
    grads.on_b(1, 0)
    chunk(5)
    grads.on_b(1, 1)
    grads.pass_on(1, True)
    grads.on_b(1, 3)
    grads.on_b(1, 2)
    grads.pass_on(1, False)
    stage2(3)
    grads.on_opposite(0)
    stage2(4)
    picked(0)
    grads.on_opposite(1)
    stage2(5)
    picked(1)
    new_rows()
    new_scores()
    for i in range(N_CHUNKS):
        stage3(i)


    gather.finish()
    grads.finish()
    for made in rs_copies + list(fac_copies.values()) + list(h_copies.values()):
        made.wait_send()


def finish(rows_ref, turned_ref, new_ref, scores_ref):
    new_ref[...] = rows_ref[...]
    scores_ref[...] = turned_ref[...].T


def body(acts, gate_pre, up_pre, hidden_cot, out_cot, proj_model, proj_hidden, stored, queries, slots):
    tokens, model = acts.shape
    hidden = gate_pre.shape[1]
    vmem = pltpu.VMEM
    dma = pltpu.SemaphoreType.DMA
    new_block, turned = pl.pallas_call(
        kernel,
        out_shape=(pltpu.VMEM((8, FEAT), BF16), pltpu.VMEM((NQ, ROWS), F32)),
        in_specs=[pl.BlockSpec(memory_space=pl.ANY)] * 9 + [pl.BlockSpec(memory_space=pltpu.SMEM)],
        out_specs=(pl.BlockSpec(memory_space=pltpu.VMEM), pl.BlockSpec(memory_space=pltpu.VMEM)),
        scratch_shapes=[
            vmem((tokens, model), BF16), vmem((tokens, hidden), BF16), vmem((tokens, hidden), BF16),
            vmem((tokens, hidden), BF16), vmem((tokens, model), BF16), vmem((RANK, model), BF16),
            vmem((RANK, hidden), BF16), vmem((4 * ROWS, FEAT), BF16), vmem((64, SHARD, FEAT), BF16),
            vmem((64, SHARD, PIECE), BF16),
            vmem((384, RANK), F32), vmem((SHARD, HALF), F32), vmem((128, FLANES), BF16), vmem((3, 32, FLANES), BF16),
            vmem((4, 48, 128), BF16), vmem((3, 48, 128), BF16), vmem((192, 128), F32),
            vmem((6, NQ, 128), BF16), vmem((6, NQ, 128), BF16),
            vmem((NQ, 128), F32), vmem((NQ, 128), F32), vmem((NQ, ROWS), F32),
            vmem((SHARD, 512), BF16), vmem((3, SHARD, 512), BF16),
            dma((12,)), dma((GATHER_COPIES,)), dma((GATHER_COPIES,)), dma((GATHER_COPIES,)), dma((GATHER_COPIES,)),
            dma((6 * N_CHUNKS,)), dma((6 * N_CHUNKS,)), dma((3,)), dma((3,)), dma((3,)), dma((3,)), dma((3,)), dma((3,)),
        ],
        compiler_params=pltpu.CompilerParams(
            collective_id=0, has_side_effects=True, vmem_limit_bytes=56 * 2**20),
    )(acts, gate_pre, up_pre, hidden_cot, out_cot, proj_model, proj_hidden, stored, queries, slots)
    return pl.pallas_call(
        finish,
        out_shape=(jax.ShapeDtypeStruct((8, FEAT), BF16), jax.ShapeDtypeStruct((ROWS, NQ), F32)),
    )(new_block, turned)


def solution(mesh):
    return jax.shard_map(
        body,
        mesh=mesh,
        in_specs=(
            P("dp", "tensor"), P("dp", "tensor"), P("dp", "tensor"), P("dp", "tensor"), P("dp", "tensor"),
            P(None, "tensor"), P(None, "tensor"), P("dp", "tensor"), P("dp", "tensor"), P("dp"),
        ),
        out_specs=(P("dp", "tensor"), P(("dp", "tensor"), None)),
        check_vma=False,
    )
```
